32 devices in a mesh: ctx: 2 (over y), tp: 16 (over z, x, core).
Axes of the slice: x: 2, y: 2, z: 4, core: 2. Of those that a mesh axis runs over, the one named last changes fastest.
Arguments:
- tokens: bfloat16 [1024, 4096], P(('ctx', 'tp')), may hold values from -6 to 6
- gate_weight: bfloat16 [4096, 16384], P(None, 'tp'), may hold values from -0.09375 to 0.09375
- input_weight: bfloat16 [4096, 16384], P(None, 'tp'), may hold values from -0.09375 to 0.09375
- state_weight: bfloat16 [4096, 2048], P(None, 'tp'), may hold values from -0.09375 to 0.09375
- step_weight: bfloat16 [4096, 256], P(None, 'tp'), may hold values from -0.09375 to 0.09375
- input_conv: float32 [5, 16384], P(None, 'tp'), may hold values from -0.5 to 0.5
- state_conv: float32 [5, 2048], P(None, 'tp'), may hold values from -0.5 to 0.5
- log_rate: float32 [256], P('tp'), may hold values from -12 to 2.1
- step_bias: float32 [256], P('tp'), may hold values from -6 to -2
- skip_gain: float32 [256], P('tp'), may hold values from 0.5 to 2
- norm_gain: float32 [16384], P('tp'), may hold values from 0.25 to 1.75
- out_weight: bfloat16 [16384, 4096], P('tp'), may hold values from -0.046875 to 0.046875
Outputs:
- mixed_out: bfloat16 [1024, 4096], P(('ctx', 'tp'))
The draws below stay inside these ranges and needn't reach their ends.
All inputs are finite; a program needn't handle non-finite values.
Results may differ from the reference program's by a relative error of at most 0.0035.
The reference program's roundings to bfloat16 on the way (of `gate_rows`, `input_rows`, `state_rows`, `conv_inputs`, `conv_states` and `normed`) count: a program that leaves them out, or rounds other values in their place, can miss the bound.
Values may be sent and summed in bfloat16 or wider, within the bound.
A program may use at most 128 MiB of HBM per device.

```python
import math
import jax
import jax.numpy as jnp
from jax import lax

D = 4096
HEADS = 256
PDIM = 64
NSTATE = 256
GROUPS = 4
CONV = 4
SPAN = 64
TOKENS = 1024
DINNER = 16384
BCW = 2048


def draw_log_rate(key, part):
    first_key, second_key, third_key = jax.random.split(key, 3)
    fast_share = 0.5
    is_fast = jax.random.uniform(first_key, (HEADS,), jnp.float32) < fast_share
    fast_rate = jnp.exp(jax.random.uniform(second_key, (HEADS,), jnp.float32, math.log(2.0), math.log(8.0)))
    slow_rate = jnp.exp(jax.random.uniform(third_key, (HEADS,), jnp.float32, math.log(0.3), math.log(1.5))) / (0.2 * TOKENS)
    return jnp.log(jnp.where(is_fast, fast_rate, slow_rate)).astype(jnp.float32)


def shard_levels(stream_key, shape, cuts, smallest, high):
    factor_of, own = 1.0, jax.random.fold_in(stream_key, 6)
    for dim, blocks in cuts:
        steps = jnp.exp(jax.random.uniform(jax.random.fold_in(own, dim), (blocks,), jnp.float32, smallest / len(cuts), high / len(cuts)))
        factor_of = factor_of * jnp.repeat(steps, shape[dim] // blocks).reshape([-1 if axis == dim else 1 for axis in range(len(shape))])
    return factor_of


def normal_values(key, dims, width, reach, cuts=(), held_as=jnp.bfloat16):
    entries = jax.random.normal(key, dims, jnp.float32) * width
    if len(cuts) > 0:
        entries = shard_levels(key, dims, cuts, -0.22, 0.18) * entries
    return jnp.clip(entries, min=-reach, max=reach).astype(held_as)


def setup_inputs(seed: int = 0) -> dict:
    splits = jax.random.split(jax.random.key(seed), 13)
    tokens = normal_values(splits[0], (TOKENS, D), 1.0, 6.0, ((0, 32),))
    gate_weight = normal_values(splits[1], (D, DINNER), D ** -0.5, 0.09375, ((1, 16),))
    input_weight = normal_values(splits[2], (D, DINNER), D ** -0.5, 0.09375, ((1, 16),))
    state_weight = normal_values(splits[3], (D, BCW), D ** -0.5, 0.09375, ((1, 16),))
    step_weight = normal_values(splits[4], (D, HEADS), D ** -0.5, 0.09375, ((1, 16),))
    input_conv = jnp.clip(jax.random.uniform(splits[5], (CONV + 1, DINNER), jnp.float32, -0.5, 0.5) * shard_levels(splits[5], (CONV + 1, DINNER), ((1, 16),), -0.4, 0.0), -0.5, 0.5)
    state_conv = jnp.clip(jax.random.uniform(splits[6], (CONV + 1, BCW), jnp.float32, -0.5, 0.5) * shard_levels(splits[6], (CONV + 1, BCW), ((1, 16),), -0.4, 0.0), -0.5, 0.5)
    log_rate = draw_log_rate(jax.random.fold_in(splits[12], 71), 0)
    step_bias = jnp.clip(-6.0 + 4.0 * jax.random.uniform(splits[8], (HEADS,), jnp.float32) ** shard_levels(splits[8], (HEADS,), ((0, 16),), -0.2, 0.2), -6.0, -2.0)
    skip_gain = jnp.clip(0.5 + 1.5 * jax.random.uniform(splits[9], (HEADS,), jnp.float32) ** shard_levels(splits[9], (HEADS,), ((0, 16),), -0.2, 0.2), 0.5, 2.0)
    norm_gain = jnp.clip(1.0 + 0.15 * jax.random.normal(splits[10], (DINNER,), jnp.float32), 0.25, 1.75)
    out_weight = normal_values(splits[11], (DINNER, D), DINNER ** -0.5, 0.046875, ((0, 16),))
    return {"tokens": tokens, "gate_weight": gate_weight, "input_weight": input_weight, "state_weight": state_weight, "step_weight": step_weight, "input_conv": input_conv, "state_conv": state_conv, "log_rate": log_rate, "step_bias": step_bias, "skip_gain": skip_gain, "norm_gain": norm_gain, "out_weight": out_weight}


def conv_silu(sequence, conv_taps):
    row_count = sequence.shape[0]
    padded = jnp.concatenate([jnp.zeros((CONV - 1, sequence.shape[1]), sequence.dtype), sequence], axis=0).astype(jnp.float32)
    running = conv_taps[CONV] + conv_taps[0] * padded[0:row_count]
    for offset in range(1, CONV):
        running = running + conv_taps[offset] * padded[offset:offset + row_count]
    return jax.nn.silu(running).astype(jnp.bfloat16)

def span_terms(inputs, step_size, log_damp, write_vec, read_vec):
    highest = lax.Precision.HIGHEST
    cumulative = jnp.cumsum(log_damp, axis=1)
    length = log_damp.shape[1]
    causal = (jnp.arange(length)[:, None] >= jnp.arange(length)[None, :])[None, :, :, None]
    scores = jnp.einsum('kin,kjn->kij', read_vec, write_vec, precision=highest)
    spread = cumulative[:, :, None, :] - cumulative[:, None, :, :]
    damping = jnp.exp(jnp.where(causal, spread, -jnp.inf))
    mixing = scores[:, :, :, None] * damping * step_size[:, None, :, :]
    within = jnp.einsum('kijh,kjhp->kihp', mixing, inputs, precision=highest)
    to_end = jnp.exp(cumulative[:, -1:, :] - cumulative) * step_size
    states = jnp.einsum('kjh,kjhp,kjn->khpn', to_end, inputs, write_vec, precision=highest)
    return (cumulative, within, states)

def span_pass(cumulative, states, read_vec, zero_state):

    def advance(carried, payload):
        factor, increment = payload
        return (factor[:, None, None] * carried + increment, carried)
    last_state, entering = lax.scan(advance, zero_state, (jnp.exp(cumulative[:, -1, :]), states))
    across = jnp.einsum('kih,kin,khpn->kihp', jnp.exp(cumulative), read_vec, entering, precision=lax.Precision.HIGHEST)
    return (last_state, across)

def reference(tokens, gate_weight, input_weight, state_weight, step_weight, input_conv, state_conv, log_rate, step_bias, skip_gain, norm_gain, out_weight):
    gate_rows = jnp.dot(tokens, gate_weight, preferred_element_type=jnp.float32).astype(jnp.bfloat16)
    input_rows = jnp.dot(tokens, input_weight, preferred_element_type=jnp.float32).astype(jnp.bfloat16)
    state_rows = jnp.dot(tokens, state_weight, preferred_element_type=jnp.float32).astype(jnp.bfloat16)
    step_raw = jnp.dot(tokens, step_weight, preferred_element_type=jnp.float32)
    conv_inputs = conv_silu(input_rows, input_conv)
    conv_states = conv_silu(state_rows, state_conv)
    step_size = jax.nn.softplus(step_raw + step_bias)
    log_damp = -step_size * jnp.exp(log_rate)
    per_group = HEADS // GROUPS
    blocks = TOKENS // SPAN
    inputs = conv_inputs.astype(jnp.float32).reshape(blocks, SPAN, GROUPS, per_group, PDIM).transpose(2, 0, 1, 3, 4)
    group_steps = step_size.reshape(blocks, SPAN, GROUPS, per_group).transpose(2, 0, 1, 3)
    group_damp = log_damp.reshape(blocks, SPAN, GROUPS, per_group).transpose(2, 0, 1, 3)
    vectors = conv_states.astype(jnp.float32).reshape(blocks, SPAN, GROUPS, 2, NSTATE).transpose(2, 3, 0, 1, 4)

    def one_group(payload):
        group_inputs, steps_here, damp_here, vectors_here = payload
        cumulative, within, states = span_terms(group_inputs, steps_here, damp_here, vectors_here[0], vectors_here[1])
        zero_state = jnp.zeros((per_group, PDIM, NSTATE), jnp.float32)
        last_state, across = span_pass(cumulative, states, vectors_here[1], zero_state)
        return within + across
    outputs = lax.map(one_group, (inputs, group_steps, group_damp, vectors))
    outputs = outputs.transpose(1, 2, 0, 3, 4).reshape(TOKENS, HEADS, PDIM)
    outputs = outputs + skip_gain[None, :, None] * conv_inputs.astype(jnp.float32).reshape(TOKENS, HEADS, PDIM)
    gate_out = outputs.reshape(TOKENS, DINNER) * jax.nn.silu(gate_rows.astype(jnp.float32))
    grouped = gate_out.reshape(TOKENS, GROUPS, DINNER // GROUPS)
    mean_square = lax.optimization_barrier(jnp.sum(grouped * grouped, axis=2)) / (DINNER // GROUPS)
    scaled = (grouped * lax.rsqrt(mean_square + 1e-05)[:, :, None]).reshape(TOKENS, DINNER)
    normed = (scaled * norm_gain).astype(jnp.bfloat16)
    return jnp.dot(normed, out_weight, preferred_element_type=jnp.float32).astype(jnp.bfloat16)
```

```python
import functools

import jax
import jax.numpy as jnp
from jax import lax
from jax.experimental import pallas as pl
from jax.experimental.pallas import tpu as pltpu
from jax.sharding import PartitionSpec as P

NSTATE = 256
GROUPS = 4
CONV = 4
DINNER = 16384
CHUNK = 128
MESH = pl.DeviceIdType.MESH
HIGH = lax.Precision.HIGHEST
F32 = jnp.float32
BF16 = jnp.bfloat16
VMEM = pl.BlockSpec(memory_space=pltpu.VMEM)
ANY = pl.BlockSpec(memory_space=pl.ANY)


def passed_along(array, axis, by):
    peers = lax.axis_size(axis)
    pairs = [(i, i + by) for i in range(peers) if 0 <= i + by < peers]
    return lax.ppermute(array, axis, pairs)


def from_partner(array, axis, distance):
    return lax.ppermute(array, axis, [(i, i ^ 1 << distance) for i in range(lax.axis_size(axis))])


def two_parts(value):
    high = value.astype(BF16)
    return high, (value - high.astype(F32)).astype(BF16)


def ssd_kernel(x_ref, bc_ref, dt_ref, la_ref, dtt_ref, lat_ref, e_ref, y_ref, st_ref, cum_ref):
    rows, width = x_ref.shape
    heads = dt_ref.shape[1]
    head_dim = width // heads
    q = CHUNK
    st_ref[...] = jnp.zeros_like(st_ref)
    row = lax.broadcasted_iota(jnp.int32, (q, q), 0)
    col = lax.broadcasted_iota(jnp.int32, (q, q), 1)
    causal = row >= col
    lower = causal.astype(F32)
    upper = (row <= col).astype(F32)
    first = lax.broadcasted_iota(jnp.int32, (q, 2 * head_dim), 1) < head_dim
    spread_out = e_ref[...]
    offset = jnp.zeros((1, heads), F32)
    for k in range(rows // q):
        at = pl.ds(k * q, q)
        cum = jnp.dot(lower, la_ref[at, :], precision=HIGH, preferred_element_type=F32)
        cumt = jnp.dot(lat_ref[:, at], upper, precision=HIGH, preferred_element_type=F32)
        cum_ref[at, :] = cum + offset
        last = cum[q - 1 : q, :]
        offset = offset + last
        dtt = dtt_ref[:, at]
        write = bc_ref[at, :NSTATE]
        read = bc_ref[at, NSTATE:]
        scores = lax.dot_general(read, write, (((1,), (1,)), ((), ())), preferred_element_type=F32)
        scores = jnp.where(causal, scores, 0.0)
        grow = jnp.dot(jnp.exp(cum), spread_out, precision=HIGH, preferred_element_type=F32)
        weight = jnp.dot(
            jnp.exp(last - cum) * dt_ref[at, :], spread_out, precision=HIGH, preferred_element_type=F32
        )
        x = x_ref[at, :]
        if k > 0:
            high, low = two_parts(st_ref[...])
            across = jnp.dot(read, high, preferred_element_type=F32)
            y_ref[at, :] = grow * (across + jnp.dot(read, low, preferred_element_type=F32))
        for h in range(0, heads, 2):
            mixes = []
            for i in (h, h + 1):
                gap = jnp.minimum(cum[:, i : i + 1] - cumt[i : i + 1, :], 0.0)
                mixes.append(scores * jnp.exp(gap) * dtt[i : i + 1, :])
            lanes = slice(h * head_dim, (h + 2) * head_dim)
            pair = x[:, lanes]
            none = jnp.zeros_like(pair)
            stacked = jnp.concatenate([jnp.where(first, pair, none), jnp.where(first, none, pair)], axis=0)
            high, low = two_parts(jnp.concatenate(mixes, axis=1))
            within = jnp.dot(high, stacked, preferred_element_type=F32)
            within = within + jnp.dot(low, stacked, preferred_element_type=F32)
            if k > 0:
                y_ref[at, lanes] += within
            else:
                y_ref[at, lanes] = within
        high, low = two_parts(x.astype(F32) * weight)
        over_rows = (((0,), (0,)), ((), ()))
        added = lax.dot_general(write, high, over_rows, preferred_element_type=F32)
        added = added + lax.dot_general(write, low, over_rows, preferred_element_type=F32)
        st_ref[...] = grow[q - 1 : q, :] * st_ref[...] + added


def gate_kernel(y_ref, cum_ref, bc_ref, inc_ref, x_ref, skip_ref, gate_ref, e_ref, go_ref, sq_ref):
    grow = jnp.dot(jnp.exp(cum_ref[...]), e_ref[...], precision=HIGH, preferred_element_type=F32)
    carried = jnp.dot(bc_ref[:, NSTATE:], inc_ref[...], preferred_element_type=F32)
    y = y_ref[...] + grow * carried + skip_ref[...] * x_ref[...].astype(F32)
    out = y * jax.nn.silu(gate_ref[...].astype(F32))
    go_ref[...] = out
    sq_ref[...] = jnp.sum(out * out, axis=1, keepdims=True)


def out_kernel(
    size_a, size_b, steps, go_ref, r_ref, gain_ref, w_hbm, o_ref,
    normed, w_ref, own, send1, recv1, send2, recv2, send3, recv3,
    w_sem, s1, r1, s2, r2, s3, r3,
):
    me = lax.axis_index("tp")
    a = me // (2 * size_b)
    b = me // 2 % size_b
    c = me % 2
    sibling = me + 1 - 2 * c
    blocks = size_a * size_b
    rows = normed.shape[0]
    part = rows // (2 * blocks)
    wide = w_ref.shape[2]

    def peer_b(i):
        return a * (2 * size_b) + (b + i) % size_b * 2 + c

    def peer_a(i):
        return (a + i) % size_a * (2 * size_b) + b * 2 + c

    def w_copy(k):
        return pltpu.make_async_copy(
            w_hbm.at[:, pl.ds(pl.multiple_of(k * wide, wide), wide)], w_ref.at[k], w_sem.at[k]
        )

    for k in range(steps):
        w_copy(k).start()
    barrier = pltpu.get_barrier_semaphore()
    pl.semaphore_signal(barrier, inc=1, device_id={"tp": sibling}, device_id_type=MESH)
    for i in range(1, size_b):
        pl.semaphore_signal(barrier, inc=1, device_id={"tp": peer_b(i)}, device_id_type=MESH)
    for i in range(1, size_a):
        pl.semaphore_signal(barrier, inc=1, device_id={"tp": peer_a(i)}, device_id_type=MESH)

    normed[...] = (go_ref[...] * r_ref[...] * gain_ref[...]).astype(BF16)
    pl.semaphore_wait(barrier, size_a + size_b - 1)

    def copy1(k):
        return pltpu.make_async_remote_copy(
            src_ref=send1.at[k], dst_ref=recv1.at[k], send_sem=s1.at[k], recv_sem=r1.at[k],
            device_id={"tp": sibling}, device_id_type=MESH,
        )

    def copy2(k, i):
        return pltpu.make_async_remote_copy(
            src_ref=send2.at[i - 1, k], dst_ref=recv2.at[i - 1, k],
            send_sem=s2.at[i - 1, k], recv_sem=r2.at[i - 1, k],
            device_id={"tp": peer_b(i)}, device_id_type=MESH,
        )

    def copy3(k, i):
        return pltpu.make_async_remote_copy(
            src_ref=send3.at[i - 1, k], dst_ref=recv3.at[i - 1, k],
            send_sem=s3.at[i - 1, k], recv_sem=r3.at[i - 1, k],
            device_id={"tp": peer_a(i)}, device_id_type=MESH,
        )

    def rows_of(core):
        return jnp.concatenate(
            [normed[pl.ds(pl.multiple_of((j * 2 + core) * part, part), part), :] for j in range(blocks)], axis=0
        )

    def step(k, carry):
        @pl.when(k < steps)
        def _():
            w_copy(k).wait()
            theirs = jnp.dot(rows_of(1 - c), w_ref[k], preferred_element_type=F32)
            send1[k] = theirs
            copy1(k).start()
            mine = jnp.dot(rows_of(c), w_ref[k], preferred_element_type=F32)
            own[k] = mine.reshape(size_a, size_b, part, wide)

        @pl.when((k >= 1) & (k < steps + 1))
        def _():
            j = k - 1
            copy1(j).wait_recv()
            own[j] += recv1[j].astype(F32).reshape(size_a, size_b, part, wide)
            for i in range(1, size_b):
                send2[i - 1, j] = own[j, :, (b + i) % size_b]
                copy2(j, i).start()

        @pl.when((k >= 2) & (k < steps + 2))
        def _():
            j = k - 2
            mine = own[j, :, b]
            for i in range(1, size_b):
                copy2(j, i).wait_recv()
                mine = mine + recv2[i - 1, j].astype(F32)
            own[j, :, b] = mine
            for i in range(1, size_a):
                send3[i - 1, j] = own[j, (a + i) % size_a, b].astype(BF16)
                copy3(j, i).start()

        @pl.when(k >= 3)
        def _():
            j = k - 3
            mine = own[j, a, b]
            for i in range(1, size_a):
                copy3(j, i).wait_recv()
                mine = mine + recv3[i - 1, j].astype(F32)
            o_ref[:, pl.ds(pl.multiple_of(j * wide, wide), wide)] = mine.astype(BF16)

        return carry

    lax.fori_loop(0, steps + 3, step, 0)

    def drain(k, carry):
        copy1(k).wait_send()
        for i in range(1, size_b):
            copy2(k, i).wait_send()
        for i in range(1, size_a):
            copy3(k, i).wait_send()
        return carry

    lax.fori_loop(0, steps, drain, 0)


def project_out(go, r, gain, weight, tp):
    rows = go.shape[0]
    depth, columns = weight.shape
    size_a = 4
    size_b = tp // (2 * size_a)
    steps = 8
    wide = columns // steps
    part = rows // tp
    half = rows // 2
    dma = pltpu.SemaphoreType.DMA
    return pl.pallas_call(
        functools.partial(out_kernel, size_a, size_b, steps),
        out_shape=jax.ShapeDtypeStruct((part, columns), BF16),
        in_specs=[VMEM, VMEM, VMEM, ANY],
        out_specs=VMEM,
        scratch_shapes=[
            pltpu.VMEM((rows, depth), BF16),
            pltpu.VMEM((steps, depth, wide), BF16),
            pltpu.VMEM((steps, size_a, size_b, part, wide), F32),
            pltpu.VMEM((steps, half, wide), F32),
            pltpu.VMEM((steps, half, wide), F32),
            pltpu.VMEM((size_b - 1, steps, size_a, part, wide), F32),
            pltpu.VMEM((size_b - 1, steps, size_a, part, wide), F32),
            pltpu.VMEM((size_a - 1, steps, part, wide), BF16),
            pltpu.VMEM((size_a - 1, steps, part, wide), BF16),
            dma((steps,)), dma((steps,)), dma((steps,)),
            dma((size_b - 1, steps)), dma((size_b - 1, steps)),
            dma((size_a - 1, steps)), dma((size_a - 1, steps)),
        ],
        compiler_params=pltpu.CompilerParams(
            collective_id=1, has_side_effects=True, vmem_limit_bytes=50 * 1024 * 1024
        ),
    )(go, r, gain, weight)


def body(
    tokens, gate_weight, input_weight, state_weight, step_weight, input_conv, state_conv,
    log_rate, step_bias, skip_gain, norm_gain, out_weight,
):
    tensor_size = lax.axis_size("tp")
    ctx_size = lax.axis_size("ctx")
    per_group = tensor_size // GROUPS
    level_count = per_group.bit_length() - 1
    my_index = lax.axis_index("tp")
    local_width = gate_weight.shape[1]
    state_width = state_weight.shape[1]
    heads = log_rate.shape[0]
    head_dim = local_width // heads
    combined = jnp.concatenate([gate_weight, input_weight, state_weight, step_weight], axis=1)
    projected = jnp.dot(
        lax.all_gather(tokens, "tp", axis=0, tiled=True), combined, preferred_element_type=F32
    )
    rows = projected.shape[0]
    gate_rows = projected[:, :local_width].astype(BF16)
    streams = projected[:, local_width : 2 * local_width + state_width].astype(BF16)
    step_raw = projected[:, 2 * local_width + state_width :]
    rim_rows = passed_along(streams[rows - CONV + 1 :], "ctx", 1)
    conv_taps = jnp.concatenate([input_conv, state_conv], axis=1)
    extended = jnp.concatenate([rim_rows, streams], axis=0)
    running = conv_taps[CONV] + conv_taps[0] * extended[0:rows].astype(F32)
    for offset in range(1, CONV):
        running = running + conv_taps[offset] * extended[offset : offset + rows].astype(F32)
    convolved = jax.nn.silu(running).astype(BF16)
    conv_inputs = convolved[:, :local_width]
    pieces = convolved[:, local_width:]
    for bit_pos in range(level_count):
        partner = from_partner(pieces, "tp", bit_pos)
        lower = my_index // (1 << bit_pos) % 2 == 0
        pieces = jnp.where(
            lower,
            jnp.concatenate([pieces, partner], axis=1),
            jnp.concatenate([partner, pieces], axis=1),
        )
    step_size = jax.nn.softplus(step_raw + step_bias)
    log_damp = -step_size * jnp.exp(log_rate)
    spread_out = jnp.repeat(jnp.eye(heads, dtype=F32), head_dim, axis=1)

    local_y, block_state, cumulative = pl.pallas_call(
        ssd_kernel,
        out_shape=(
            jax.ShapeDtypeStruct((rows, local_width), F32),
            jax.ShapeDtypeStruct((NSTATE, local_width), F32),
            jax.ShapeDtypeStruct((rows, heads), F32),
        ),
        in_specs=[VMEM] * 7,
        out_specs=(VMEM, VMEM, VMEM),
        compiler_params=pltpu.CompilerParams(vmem_limit_bytes=40 * 1024 * 1024),
    )(conv_inputs, pieces, step_size, log_damp, step_size.T, log_damp.T, spread_out)

    sent_state = block_state.astype(BF16)
    if ctx_size == 2:
        incoming = passed_along(sent_state, "ctx", 1)
    else:
        damps = lax.all_gather(jnp.repeat(jnp.exp(cumulative[-1]), head_dim), "ctx")
        states = lax.all_gather(sent_state, "ctx")

        def one(hop, state):
            return damps[hop][None, :] * state + states[hop].astype(F32)

        incoming = lax.fori_loop(
            0, lax.axis_index("ctx"), one, jnp.zeros((NSTATE, local_width), F32)
        ).astype(BF16)

    def by_rows(width):
        return pl.BlockSpec((CHUNK, width), lambda i: (i, 0))

    def whole(array):
        return pl.BlockSpec(array.shape, lambda i: (0, 0))

    skip = jnp.repeat(skip_gain, head_dim)[None, :]
    gate_out, square_sum = pl.pallas_call(
        gate_kernel,
        grid=(rows // CHUNK,),
        out_shape=(
            jax.ShapeDtypeStruct((rows, local_width), F32),
            jax.ShapeDtypeStruct((rows, 1), F32),
        ),
        in_specs=[
            by_rows(local_width), by_rows(heads), by_rows(2 * NSTATE), whole(incoming),
            by_rows(local_width), whole(skip), by_rows(local_width), whole(spread_out),
        ],
        out_specs=(by_rows(local_width), by_rows(1)),
        compiler_params=pltpu.CompilerParams(vmem_limit_bytes=40 * 1024 * 1024),
    )(local_y, cumulative, pieces, incoming, conv_inputs, skip, gate_rows, spread_out)
    square_sum = square_sum[:, 0]
    for bit_pos in range(level_count):
        square_sum = square_sum + from_partner(square_sum, "tp", bit_pos)
    mean_square = square_sum / (DINNER // GROUPS)
    inverse = lax.rsqrt(mean_square + 1e-05)[:, None]
    return project_out(gate_out, inverse, norm_gain[None, :], out_weight, tensor_size)


def solution(mesh):
    placed = (
        P(("ctx", "tp"), None),
        P(None, "tp"),
        P(None, "tp"),
        P(None, "tp"),
        P(None, "tp"),
        P(None, "tp"),
        P(None, "tp"),
        P("tp"),
        P("tp"),
        P("tp"),
        P("tp"),
        P("tp", None),
    )
    return jax.shard_map(
        body, mesh=mesh, in_specs=placed, out_specs=P(("ctx", "tp"), None), check_vma=False
    )
```
